256 devices in a mesh: leaf: 64 (over x, z, core), rhs: 4 (over y).
Axes of the slice: x: 4, y: 4, z: 8, core: 2. Of those that a mesh axis runs over, the one named last changes fastest.
Arguments:
- values: float32 [16, 524288], P('rhs', 'leaf'), may hold values from -6 to 6
- geometry: float32 [7, 524288], P(None, ('leaf', 'rhs')), may hold values from -5 to 414, as said below
- basis: float32 [4096, 32, 128], P(('leaf', 'rhs')), may hold values from -0.5 to 0.5
- near: int32 [4096, 6], P('leaf'), may hold values from -1 to 4095, as said below
- transfer_one: float32 [2048, 2048], P('leaf'), may hold values from -0.75 to 0.75
- transfer_two: float32 [1024, 2048], P('leaf'), may hold values from -0.75 to 0.75
- couple_one: float32 [2048, 8192], P('leaf'), may hold values from -0.375 to 0.375
- couple_two: float32 [1024, 8192], P('leaf'), may hold values from -0.375 to 0.375
- lists_one: int32 [2048, 8], P('leaf'), may hold values from -1 to 2047, as said below
- lists_two: int32 [1024, 8], P('leaf'), may hold values from -1 to 1023, as said below
Outputs:
- applied: float32 [16, 524288], P('rhs', 'leaf')
The draws below stay inside these ranges and needn't reach their ends.
Inputs may be any that keep to these rules, and one draw needn't show every extreme that they name: `geometry`: rows 0 to 2 are positions, rows 3 to 5 normal vectors not of unit length, row 6 positive weights. `near`: entry [i, j] is -1 (no partner) or a leaf within 16 leaves of i, and that distance is reached; entry [i, 0] is i; entries may repeat. `lists_one`: entry [t, j] is -1 (no partner) or a cluster of level one within 4 clusters of t, and that distance is reached; entries may repeat. `lists_two`: entry [t, j] is -1 (no partner) or any cluster of level two; entry [t, 0] is never -1; entries may repeat.
All inputs are finite; a program needn't handle non-finite values.
Results may differ from the reference program's by a relative error of at most 0.0003.
Values sent between devices are 32-bit elements; how exact they have to be, the bound alone decides.
No kernel may reach another device: no remote copies, remote signals or barrier semaphores. Data moves between devices by JAX's collectives and lax.ppermute only.
A program may use at most 192 MiB of HBM per device.

```python
import jax
import jax.numpy as jnp
from jax import lax

PTS = 128
RANK = 32
RHS = 16
LEAF_DEV = 64
NEAR = 6
COUPLE = 8
HALO = 16
BAND = 4
LEAVES = 4096
POINTS = 524288
CL1 = 2048
CL2 = 1024


def draw_geometry(key, part):
    key = jax.random.fold_in(key, 7)
    key_shift, key_normal, key_weight = jax.random.split(key, 3)
    leaf_pos = (jnp.arange(POINTS) // PTS).astype(jnp.float32)
    centers = jnp.stack([2.0 * jnp.cos(0.3 * leaf_pos), 2.0 * jnp.sin(0.3 * leaf_pos), 0.1 * leaf_pos])
    shifts = jnp.clip(0.6 * jax.random.normal(key_shift, (3, POINTS), jnp.float32), -2.4, 2.4)
    normals = jax.random.uniform(key_normal, (3, POINTS), jnp.float32, -1.0, 1.0)
    spread = jax.random.uniform(key_weight, (POINTS,), jnp.float32, -0.69, 0.69)
    weights = 0.5 * jnp.exp(spread) / jnp.sqrt(jnp.float32(PTS))
    return jnp.concatenate([centers + shifts, normals, weights[None, :]], axis=0).astype(jnp.float32)


def draw_near(key, part):
    key = jax.random.fold_in(key, 11)
    key_offs, key_heavy, key_chosen, key_count = jax.random.split(key, 4)
    rows_all = jnp.arange(LEAVES)
    offsets = jax.random.randint(key_offs, (LEAVES, NEAR), -HALO, HALO + 1)
    offsets = offsets.at[:, 0].set(0)
    devices = LEAVES // LEAF_DEV
    heavy = jax.random.randint(key_heavy, (devices,), 0, 4) == 0
    chosen = jax.random.randint(key_chosen, (), 0, devices)
    heavy = heavy | (jnp.arange(devices) == chosen)
    light = jax.random.randint(key_count, (LEAVES,), 1, NEAR // 2 + 1)
    amounts = jnp.where(heavy[rows_all // LEAF_DEV], NEAR, light)
    source = rows_all[:, None] + offsets
    usable = (jnp.arange(NEAR)[None, :] < amounts[:, None]) & (source >= 0) & (source < LEAVES)
    result = jnp.where(usable, source, -1)
    result = result.at[0, 1].set(HALO)
    return result.astype(jnp.int32)


def draw_lists_one(key, part):
    key = jax.random.fold_in(key, 13)
    key_offs, key_count = jax.random.split(key, 2)
    rows_all = jnp.arange(CL1)
    offsets = jax.random.randint(key_offs, (CL1, COUPLE), -BAND, BAND + 1)
    amounts = jax.random.randint(key_count, (CL1,), 2, COUPLE + 1)
    source = rows_all[:, None] + offsets
    usable = (jnp.arange(COUPLE)[None, :] < amounts[:, None]) & (source >= 0) & (source < CL1)
    result = jnp.where(usable, source, -1)
    result = result.at[0, 1].set(BAND)
    result = result.at[CL1 - 1, 0].set(CL1 - 1)
    result = result.at[CL1 - 1, COUPLE - 1].set(-1)
    return result.astype(jnp.int32)


def draw_lists_two(key, part):
    key = jax.random.fold_in(key, 17)
    key_index, key_count = jax.random.split(key, 2)
    targets = jax.random.randint(key_index, (CL2, COUPLE), 0, CL2)
    amounts = jax.random.randint(key_count, (CL2,), 1, COUPLE + 1)
    usable = jnp.arange(COUPLE)[None, :] < amounts[:, None]
    result = jnp.where(usable, targets, -1)
    result = result.at[0, 0].set(CL2 - 1)
    return result.astype(jnp.int32)


def steps_of(rng, shape, pieces, low, largest):
    factor_of, own = 1.0, jax.random.fold_in(rng, 6)
    for dim, blocks in pieces:
        heights = jnp.exp(jax.random.uniform(jax.random.fold_in(own, dim), (blocks,), jnp.float32, low / len(pieces), largest / len(pieces)))
        factor_of = factor_of * jnp.repeat(heights, shape[dim] // blocks).reshape([-1 if axis == dim else 1 for axis in range(len(shape))])
    return factor_of


def normal_values(stream_key, dims, width, limit, cuts=(), held_as=jnp.bfloat16):
    values = jax.random.normal(stream_key, dims, jnp.float32) * width
    if len(cuts) > 0:
        values = steps_of(stream_key, dims, cuts, -0.22, 0.18) * values
    return jnp.clip(values, min=-limit, max=limit).astype(held_as)


def setup_inputs(seed: int = 0) -> dict:
    splits = jax.random.split(jax.random.key(seed), 11)
    return {
        "values": normal_values(splits[0], (RHS, POINTS), 1.0, 6.0, ((0, 4), (1, 64)), jnp.float32),
        "geometry": draw_geometry(jax.random.fold_in(splits[10], 71), 0),
        "basis": normal_values(splits[2], (LEAVES, RANK, PTS), PTS ** -0.5, 0.5, ((0, 256),), jnp.float32),
        "near": draw_near(jax.random.fold_in(splits[10], 71), 0),
        "transfer_one": normal_values(splits[4], (CL1, 2 * RANK * RANK), (2 * RANK) ** -0.5, 0.75, ((0, 64),), jnp.float32),
        "transfer_two": normal_values(splits[5], (CL2, 2 * RANK * RANK), (2 * RANK) ** -0.5, 0.75, ((0, 64),), jnp.float32),
        "couple_one": normal_values(splits[6], (CL1, COUPLE * RANK * RANK), (COUPLE * RANK) ** -0.5, 0.375, ((0, 64),), jnp.float32),
        "couple_two": normal_values(splits[7], (CL2, COUPLE * RANK * RANK), (COUPLE * RANK) ** -0.5, 0.375, ((0, 64),), jnp.float32),
        "lists_one": draw_lists_one(jax.random.fold_in(splits[10], 71), 0),
        "lists_two": draw_lists_two(jax.random.fold_in(splits[10], 71), 0),
    }


SOFTEN = 0.05
CONTRAST = 0.6
HIGHEST = lax.Precision.HIGHEST

def kernel_apply(target_geo, source_geo, source_val):
    separation = target_geo[0:3, :, :, None] - source_geo[0:3, :, None, :]
    distance = lax.optimization_barrier(jnp.sum(separation * separation, axis=0)) + SOFTEN
    inverse = 1.0 / jnp.sqrt(distance)
    normal_term = lax.optimization_barrier(jnp.sum(source_geo[3:6, :, None, :] * separation, axis=0)) * inverse ** 3
    kernel = source_geo[6][:, None, :] * (inverse + CONTRAST * normal_term)
    return jnp.einsum('tps,rts->rtp', kernel, source_val, precision=HIGHEST)

def blockwise(target_geo, source_geo, source_val):
    groups = LEAVES // 32

    def split_up(array):
        return jnp.moveaxis(array.reshape(array.shape[0], groups, 32, PTS), 1, 0)

    def one_block(triple):
        return kernel_apply(triple[0], triple[1], triple[2])
    result = lax.map(one_block, (split_up(target_geo), split_up(source_geo), split_up(source_val)))
    return jnp.moveaxis(result, 0, 1).reshape(RHS, LEAVES, PTS)

def reference(values, geometry, basis, near, transfer_one, transfer_two, couple_one, couple_two, lists_one, lists_two):
    geo_all = geometry.reshape(7, LEAVES, PTS)
    vals_all = values.reshape(RHS, LEAVES, PTS)
    near_part = jnp.zeros((RHS, LEAVES, PTS), jnp.float32)
    for slot_index in range(NEAR):
        source = near[:, slot_index]
        inside = (source >= 0).astype(jnp.float32)
        picked = jnp.clip(source, 0, LEAVES - 1).astype(jnp.int32)
        source_geo = geo_all[:, picked]
        source_val = vals_all[:, picked] * inside[None, :, None]
        near_part = near_part + blockwise(geo_all, source_geo, source_val)
    coef_leaf = jnp.einsum('lkp,rlp->rlk', basis, vals_all, precision=HIGHEST)
    lift_one = transfer_one.reshape(CL1, 2, RANK, RANK)
    lift_two = transfer_two.reshape(CL2, 2, RANK, RANK)
    coef_one = jnp.einsum('tkab,rtkb->rta', lift_one, coef_leaf.reshape(RHS, CL1, 2, RANK), precision=HIGHEST)
    coef_two = jnp.einsum('tkab,rtkb->rta', lift_two, coef_one.reshape(RHS, CL2, 2, RANK), precision=HIGHEST)
    mats_one = couple_one.reshape(CL1, COUPLE, RANK, RANK)
    mats_two = couple_two.reshape(CL2, COUPLE, RANK, RANK)
    live_one = (lists_one >= 0).astype(jnp.float32)
    fetched_one = coef_one[:, jnp.clip(lists_one, 0, CL1 - 1).astype(jnp.int32)] * live_one[None, :, :, None]
    down_one = jnp.einsum('tjab,rtjb->rta', mats_one, fetched_one, precision=HIGHEST)
    live_two = (lists_two >= 0).astype(jnp.float32)
    fetched_two = coef_two[:, jnp.clip(lists_two, 0, CL2 - 1).astype(jnp.int32)] * live_two[None, :, :, None]
    down_two = jnp.einsum('tjab,rtjb->rta', mats_two, fetched_two, precision=HIGHEST)
    down_mid = down_one + jnp.einsum('tkab,rta->rtkb', lift_two, down_two, precision=HIGHEST).reshape(RHS, CL1, RANK)
    down_leaf = jnp.einsum('tkab,rta->rtkb', lift_one, down_mid, precision=HIGHEST).reshape(RHS, LEAVES, RANK)
    far_part = jnp.einsum('lkp,rlk->rlp', basis, down_leaf, precision=HIGHEST)
    return (near_part + far_part).reshape(RHS, POINTS)
```

```python
import jax
import jax.numpy as jnp
from jax import lax
from jax.experimental import pallas as pl
from jax.experimental.pallas import tpu as pltpu
from jax.sharding import Mesh
from jax.sharding import PartitionSpec as P

PTS = 128
RANK = 32
NEAR = 6
COUPLE = 8
SOFTEN = 0.05
CONTRAST = 0.6
ROWS = 16
OWN = 16
F32 = jnp.float32
BF16 = jnp.bfloat16
ALL = ("x", "z", "c", "r")
VMEM = pl.BlockSpec(memory_space=pltpu.VMEM)
SMEM = pl.BlockSpec(memory_space=pltpu.SMEM)
PARAMS = pltpu.CompilerParams(vmem_limit_bytes=40 * 1024 * 1024)


def split(x):
    high = x.astype(BF16)
    return high, (x - high.astype(F32)).astype(BF16)


def dot(a, b):
    return jnp.dot(a, b, preferred_element_type=F32)


def dot_two(x, ones):
    high, low = split(x)
    return dot(high, ones) + dot(low, ones)


def lane_segment(rows):
    return lax.broadcasted_iota(jnp.int32, (rows, PTS), 1) // RANK


def fold(x):
    x = x + pltpu.roll(x, 64, 1)
    return x + pltpu.roll(x, 32, 1)


def summing():
    rows = lax.broadcasted_iota(jnp.int32, (1024, PTS), 0) // RANK
    lanes = lax.broadcasted_iota(jnp.int32, (1024, PTS), 1) % RANK
    return (rows == lanes).astype(F32).astype(BF16)


def spreading(segments):
    rows = lax.broadcasted_iota(jnp.int32, (PTS, 1024), 0)
    lanes = lax.broadcasted_iota(jnp.int32, (PTS, 1024), 1) // RANK
    return ((rows % RANK == lanes) & (rows < segments * RANK)).astype(F32).astype(BF16)


def pick(packed, segment, slot):
    return fold(jnp.where(segment == slot, packed, 0.0))


def own_half(ref, rank):
    return pltpu.roll(ref[0], (rank % 2) * 4, 0)


def up_kernel(place, v_ref, basis_ref, one_ref, two_ref, first_ref, last_ref, top_ref, leaf_c, one_c, sums, two_rows):
    rank = place[0]
    two_rows[...] = own_half(two_ref, rank)
    segment = lane_segment(ROWS)
    ones = summing()
    zeros = jnp.zeros((2 * RANK, PTS), BF16)
    for leaf in range(OWN):
        vh, vl = split(v_ref[:, leaf * PTS : (leaf + 1) * PTS])
        bh, bl = split(basis_ref[leaf])
        prod = lax.dot_general(
            jnp.concatenate([vh, vl], 0),
            jnp.concatenate([bh, bl, zeros], 0),
            (((1,), (1,)), ((), ())),
            preferred_element_type=F32,
        )
        leaf_c[leaf] = fold(prod[:ROWS] + prod[ROWS:])
    for t in range(8):
        for g in range(8):
            low, high = slice(g * PTS, (g + 1) * PTS), slice(1024 + g * PTS, 1024 + (g + 1) * PTS)
            sums[t * ROWS : (t + 1) * ROWS, low] = (
                one_ref[t : t + 1, low] * leaf_c[2 * t] + one_ref[t : t + 1, high] * leaf_c[2 * t + 1]
            )
    one_c[...] = dot_two(sums[...], ones)
    first = jnp.zeros((ROWS, PTS), F32)
    last = jnp.zeros((ROWS, PTS), F32)
    for t in range(4):
        first = jnp.where(segment == t, one_c[t * ROWS : (t + 1) * ROWS], first)
        last = jnp.where(segment == t, one_c[(t + 4) * ROWS : (t + 5) * ROWS], last)
    first_ref[...] = first
    last_ref[...] = last
    for t in range(4):
        for g in range(8):
            low, high = slice(g * PTS, (g + 1) * PTS), slice(1024 + g * PTS, 1024 + (g + 1) * PTS)
            sums[t * ROWS : (t + 1) * ROWS, low] = (
                two_rows[t : t + 1, low] * one_c[2 * t * ROWS : (2 * t + 1) * ROWS]
                + two_rows[t : t + 1, high] * one_c[(2 * t + 1) * ROWS : (2 * t + 2) * ROWS]
            )
    two = dot_two(sums[: 4 * ROWS], ones)
    top = jnp.zeros((ROWS, PTS), F32)
    for t in range(4):
        top = jnp.where(segment == t, two[t * ROWS : (t + 1) * ROWS], top)
    for copy in range(top_ref.shape[0]):
        top_ref[copy] = top


def couple_kernel(place, lists, mine_ref, other_ref, mats_ref, out0, out1, out2, out3, table, sums):
    rank, core = place[0], place[1]
    segment = lane_segment(ROWS)
    half = mine_ref.shape[0]
    table[:half] = mine_ref[...]
    table[half:] = other_ref[...]

    def body(block, _):
        for t in range(8):
            target = block * 8 + t
            step = target ^ (rank * 4)
            acc = [None] * 8
            for j in range(COUPLE):
                n = lists[target, j]
                live = (n >= 0) & (((n >> 2) & 3) == rank)
                group = jnp.where(live, n >> 4, 0)
                slot = jnp.where(live, n & 3, -1)
                coef = pick(table[((group & 1) ^ core) * half + (group >> 1)], segment, slot)
                for g in range(8):
                    row = mats_ref[block, t : t + 1, j * 1024 + g * PTS : j * 1024 + (g + 1) * PTS]
                    acc[g] = row * coef if j == 0 else acc[g] + row * coef
            for g in range(8):
                sums[pl.ds(pl.multiple_of(step * ROWS, ROWS), ROWS), g * PTS : (g + 1) * PTS] = acc[g]
        return 0

    lax.fori_loop(0, 2, body, 0)
    total = dot_two(sums[...], summing())
    for part, out in enumerate((out0, out1, out2, out3)):
        packed = jnp.zeros((ROWS, PTS), F32)
        for t in range(4):
            at = (part * 4 + t) * ROWS
            packed = jnp.where(segment == t, total[at : at + ROWS], packed)
        out[...] = packed


def near_kernel(place, near, g_left, g_own, g_right, v_left, v_own, v_right, out_ref, geo, weights):
    rank, base = place[0], place[2] * OWN - OWN
    zeros = jnp.zeros((PTS, ROWS), BF16)
    for s in range(3 * OWN):
        which, at = divmod(s, OWN)
        g_ref, v_ref = ((g_left, v_left), (g_own, v_own), (g_right, v_right))[which]
        cut = slice(at * PTS, (at + 1) * PTS)
        geo[s, 0:3] = g_ref[0:3, cut]
        geo[s, 3:6] = g_ref[3:6, cut] * CONTRAST
        scaled = v_ref[:, cut] * g_ref[6:7, cut]
        high = scaled.astype(BF16).astype(F32)
        turned = jnp.transpose(jnp.concatenate([high, scaled - high], 0)).astype(BF16)
        weights[s, 0:PTS] = turned
        weights[s, PTS : 2 * PTS] = jnp.concatenate([turned[:, :ROWS], zeros], 1)
    geo[3 * OWN] = jnp.zeros((8, PTS), F32)
    weights[3 * OWN] = jnp.zeros((2 * PTS, 2 * ROWS), BF16)

    def body(i, _):
        own = jnp.transpose(geo[OWN + i])
        px = jnp.broadcast_to(own[:, 0:1], (PTS, PTS))
        py = jnp.broadcast_to(own[:, 1:2], (PTS, PTS))
        pz = jnp.broadcast_to(own[:, 2:3], (PTS, PTS))
        total = jnp.zeros((PTS, 2 * ROWS), F32)
        for j in range(NEAR):
            n = near[rank * OWN + i, j]
            s = jnp.where(n >= 0, jnp.clip(n - base, 0, 3 * OWN - 1), 3 * OWN)
            src = geo[s]
            dx, dy, dz = px - src[0:1], py - src[1:2], pz - src[2:3]
            inv = lax.rsqrt(dx * dx + dy * dy + dz * dz + SOFTEN)
            turn = dx * src[3:4] + dy * src[4:5] + dz * src[5:6]
            value = inv + turn * (inv * inv * inv)
            high, low = split(value)
            total = total + dot(jnp.concatenate([high, low], 1), weights[s])
        flat = jnp.transpose(total)
        out_ref[:, pl.ds(pl.multiple_of(i * PTS, PTS), PTS)] = flat[:ROWS] + flat[ROWS:]
        return 0

    lax.fori_loop(0, OWN, body, 0)


def final_kernel(
    place, lists, part0, part1, part2, part3, left, first, last, right,
    one_ref, two_ref, mats_ref, basis_ref, near_ref, out_ref, table, sums, spread, two_rows,
):
    rank, base = place[0], place[2] * 8 - 4
    two_rows[...] = own_half(two_ref, rank)
    segment = lane_segment(ROWS)
    for at, ref in enumerate((left, first, last, right)):
        table[at] = ref[...]

    for t in range(8):
        acc = [None] * 8
        for j in range(COUPLE):
            n = lists[rank * 8 + t, j]
            q = jnp.clip(n - base, 0, 15)
            slot = jnp.where(n >= 0, q & 3, -1)
            coef = pick(table[q >> 2], segment, slot)
            for g in range(8):
                row = mats_ref[t : t + 1, j * 1024 + g * PTS : j * 1024 + (g + 1) * PTS]
                acc[g] = row * coef if j == 0 else acc[g] + row * coef
        for g in range(8):
            sums[t * ROWS : (t + 1) * ROWS, g * PTS : (g + 1) * PTS] = acc[g]
    mid = dot_two(sums[...], summing())
    down = part0[...] + part1[...] + part2[...] + part3[...]
    rows = jnp.concatenate([jnp.where(segment == t, down, 0.0) for t in range(4)], 0)
    spread[: 4 * ROWS] = dot_two(rows, spreading(4))
    mids = []
    for t in range(4):
        for k in range(2):
            acc = None
            for g in range(8):
                lanes = slice(g * PTS, (g + 1) * PTS)
                row = two_rows[t : t + 1, k * 1024 + g * PTS : k * 1024 + (g + 1) * PTS]
                term = row * spread[t * ROWS : (t + 1) * ROWS, lanes]
                acc = term if g == 0 else acc + term
            at = (2 * t + k) * ROWS
            mids.append(mid[at : at + ROWS] + fold(acc))
    spread[...] = dot_two(jnp.concatenate(mids, 0), spreading(1))
    zeros = jnp.zeros((RANK, PTS), BF16)
    for t in range(8):
        for k in range(2):
            acc = None
            for g in range(8):
                lanes = slice(g * PTS, (g + 1) * PTS)
                row = one_ref[t : t + 1, k * 1024 + g * PTS : k * 1024 + (g + 1) * PTS]
                term = row * spread[t * ROWS : (t + 1) * ROWS, lanes]
                acc = term if g == 0 else acc + term
            down_leaf = fold(acc)
            leaf = 2 * t + k
            high = down_leaf.astype(BF16).astype(F32)
            low = down_leaf - high
            lhs = jnp.where(segment == 1, low, jnp.where(segment == 3, 0.0, high)).astype(BF16)
            bh, bl = split(basis_ref[leaf])
            far = dot(lhs, jnp.concatenate([bh, bh, bl, zeros], 0))
            cut = slice(leaf * PTS, (leaf + 1) * PTS)
            out_ref[:, cut] = near_ref[:, cut] + far


def shape(*dims):
    return jax.ShapeDtypeStruct(dims, F32)


def on_device(values, geometry, basis, near, transfer_one, transfer_two, couple_one, couple_two, lists_one, lists_two):
    size = lax.axis_size("x") * lax.axis_size("z") * lax.axis_size("c") * lax.axis_size("r")
    gathered = lax.axis_size("x") * lax.axis_size("z")
    place = jnp.stack([lax.axis_index("r"), lax.axis_index("c"), lax.axis_index(ALL)]).astype(jnp.int32)
    up_by_one = [(i, i + 1) for i in range(size - 1)]
    down_by_one = [(i + 1, i) for i in range(size - 1)]

    def both(low, high):
        return lax.ppermute(high, ALL, up_by_one), lax.ppermute(low, ALL, down_by_one)

    geo_left, geo_right = both(geometry, geometry)
    val = lax.all_to_all(values, "r", split_axis=1, concat_axis=0, tiled=True)
    val_left, val_right = both(val, val)

    def rows_of(height, width):
        return pl.BlockSpec((height, width), lambda i, place: (place[0], 0))

    def whole(*dims):
        return pl.BlockSpec(dims, lambda i, place: (0,) * len(dims))

    two_of = pl.BlockSpec((1, 8, 2048), lambda i, place: (place[0] // 2, 0, 0))
    transfer_two = transfer_two.reshape(2, 8, 2048)
    couple_two = couple_two.reshape(2, 8, 8192)

    first, last, top = pl.pallas_call(
        up_kernel,
        grid_spec=pltpu.PrefetchScalarGridSpec(
            num_scalar_prefetch=1,
            grid=(1,),
            in_specs=[whole(ROWS, OWN * PTS), whole(OWN, RANK, PTS), rows_of(8, 2048), two_of],
            out_specs=[whole(ROWS, PTS), whole(ROWS, PTS), whole(gathered, ROWS, PTS)],
            scratch_shapes=[
                pltpu.VMEM((OWN, ROWS, PTS), F32),
                pltpu.VMEM((8 * ROWS, PTS), F32),
                pltpu.VMEM((8 * ROWS, 1024), F32),
                pltpu.VMEM((8, 2048), F32),
            ],
        ),
        out_shape=[shape(ROWS, PTS), shape(ROWS, PTS), shape(gathered, ROWS, PTS)],
        compiler_params=PARAMS,
        cost_estimate=pl.CostEstimate(flops=40_000_000, bytes_accessed=600_000, transcendentals=0),
    )(place, val, basis, transfer_one, transfer_two)

    mine = lax.all_to_all(top, ("x", "z"), split_axis=0, concat_axis=0, tiled=True)
    other = lax.ppermute(mine, "c", [(0, 1), (1, 0)])
    left, right = both(first, last)

    parts = pl.pallas_call(
        couple_kernel,
        in_specs=[SMEM, SMEM, VMEM, VMEM, VMEM],
        out_specs=[VMEM] * 4,
        out_shape=[shape(ROWS, PTS)] * 4,
        scratch_shapes=[pltpu.VMEM((2 * gathered, ROWS, PTS), F32), pltpu.VMEM((16 * ROWS, 1024), F32)],
        compiler_params=PARAMS,
        cost_estimate=pl.CostEstimate(flops=100_000_000, bytes_accessed=1_000_000, transcendentals=0),
    )(place, lists_two, mine, other, couple_two)
    received = [parts[0]]
    for s in range(1, 4):
        received.append(lax.ppermute(parts[s], "r", [(i, i ^ s) for i in range(4)]))

    near_part = pl.pallas_call(
        near_kernel,
        in_specs=[SMEM, SMEM] + [VMEM] * 6,
        out_specs=VMEM,
        out_shape=shape(ROWS, OWN * PTS),
        scratch_shapes=[
            pltpu.VMEM((3 * OWN + 1, 8, PTS), F32),
            pltpu.VMEM((3 * OWN + 1, 2 * PTS, 2 * ROWS), BF16),
        ],
        compiler_params=PARAMS,
        cost_estimate=pl.CostEstimate(flops=3_000_000_000, bytes_accessed=700_000, transcendentals=1_600_000),
    )(place, near, geo_left, geometry, geo_right, val_left, val, val_right)

    result = pl.pallas_call(
        final_kernel,
        grid_spec=pltpu.PrefetchScalarGridSpec(
            num_scalar_prefetch=1,
            grid=(1,),
            in_specs=[SMEM]
            + [whole(ROWS, PTS)] * 8
            + [rows_of(8, 2048), two_of, rows_of(8, 8192), whole(OWN, RANK, PTS), whole(ROWS, OWN * PTS)],
            out_specs=whole(ROWS, OWN * PTS),
            scratch_shapes=[
                pltpu.VMEM((4, ROWS, PTS), F32),
                pltpu.VMEM((8 * ROWS, 1024), F32),
                pltpu.VMEM((8 * ROWS, 1024), F32),
                pltpu.VMEM((8, 2048), F32),
            ],
        ),
        out_shape=shape(ROWS, OWN * PTS),
        compiler_params=PARAMS,
        cost_estimate=pl.CostEstimate(flops=40_000_000, bytes_accessed=1_000_000, transcendentals=0),
    )(
        place, lists_one, *received, left, first, last, right,
        transfer_one, transfer_two, couple_one, basis, near_part,
    )
    return lax.all_to_all(result, "r", split_axis=0, concat_axis=1, tiled=True)


def solution(mesh):
    fine = Mesh(mesh.devices.reshape(4, 8, 2, 4), ALL)
    leaf = ("x", "z", "c")
    return jax.shard_map(
        on_device,
        mesh=fine,
        in_specs=(
            P("r", leaf),
            P(None, ALL),
            P(ALL, None, None),
            P(leaf, None),
            P(leaf, None),
            P(leaf, None),
            P(leaf, None),
            P(leaf, None),
            P(leaf, None),
            P(leaf, None),
        ),
        out_specs=P("r", leaf),
        check_vma=False,
    )
```

```python
import jax
import jax.numpy as jnp
from jax import lax
from jax.experimental import pallas as pl
from jax.experimental.pallas import tpu as pltpu
from jax.sharding import Mesh
from jax.sharding import PartitionSpec as P

PTS = 128
RANK = 32
NEAR = 6
COUPLE = 8
SOFTEN = 0.05
CONTRAST = 0.6
ROWS = 16
OWN = 16
FIRST = slice(OWN * PTS, OWN * PTS + PTS)
LAST = slice(OWN * PTS + PTS, OWN * PTS + 2 * PTS)
STRIP = (ROWS + 8, OWN * PTS + 2 * PTS)
F32 = jnp.float32
BF16 = jnp.bfloat16
ALL = ("x", "z", "c", "r")
VMEM = pl.BlockSpec(memory_space=pltpu.VMEM)
SMEM = pl.BlockSpec(memory_space=pltpu.SMEM)
PARAMS = pltpu.CompilerParams(vmem_limit_bytes=40 * 1024 * 1024)


def split(x):
    high = x.astype(BF16)
    return high, (x - high.astype(F32)).astype(BF16)


def dot(a, b):
    return jnp.dot(a, b, preferred_element_type=F32)


def dot_two(x, ones):
    high, low = split(x)
    return dot(high, ones) + dot(low, ones)


def lane_segment(rows):
    return lax.broadcasted_iota(jnp.int32, (rows, PTS), 1) // RANK


def fold(x):
    x = x + pltpu.roll(x, 64, 1)
    return x + pltpu.roll(x, 32, 1)


def summing():
    rows = lax.broadcasted_iota(jnp.int32, (1024, PTS), 0) // RANK
    lanes = lax.broadcasted_iota(jnp.int32, (1024, PTS), 1) % RANK
    return (rows == lanes).astype(F32).astype(BF16)


def spreading(segments):
    rows = lax.broadcasted_iota(jnp.int32, (PTS, 1024), 0)
    lanes = lax.broadcasted_iota(jnp.int32, (PTS, 1024), 1) // RANK
    return ((rows % RANK == lanes) & (rows < segments * RANK)).astype(F32).astype(BF16)


def pick(packed, segment, slot):
    return fold(jnp.where(segment == slot, packed, 0.0))


def own_half(ref, rank):
    return pltpu.roll(ref[0], (rank % 2) * 4, 0)


def up_kernel(place, v_ref, geo_ref, basis_ref, one_ref, two_ref, strip_ref, top_ref, leaf_c, one_c, sums, two_rows):
    rank = place[0]
    two_rows[...] = own_half(two_ref, rank)
    strip_ref[:ROWS, : OWN * PTS] = v_ref[...]
    strip_ref[ROWS : ROWS + 7, : OWN * PTS] = geo_ref[...]
    segment = lane_segment(ROWS)
    ones = summing()
    zeros = jnp.zeros((2 * RANK, PTS), BF16)
    for leaf in range(OWN):
        vh, vl = split(v_ref[:, leaf * PTS : (leaf + 1) * PTS])
        bh, bl = split(basis_ref[leaf])
        prod = lax.dot_general(
            jnp.concatenate([vh, vl], 0),
            jnp.concatenate([bh, bl, zeros], 0),
            (((1,), (1,)), ((), ())),
            preferred_element_type=F32,
        )
        leaf_c[leaf] = fold(prod[:ROWS] + prod[ROWS:])
    for t in range(8):
        for g in range(8):
            low, high = slice(g * PTS, (g + 1) * PTS), slice(1024 + g * PTS, 1024 + (g + 1) * PTS)
            sums[t * ROWS : (t + 1) * ROWS, low] = (
                one_ref[t : t + 1, low] * leaf_c[2 * t] + one_ref[t : t + 1, high] * leaf_c[2 * t + 1]
            )
    one_c[...] = dot_two(sums[...], ones)
    first = jnp.zeros((ROWS, PTS), F32)
    last = jnp.zeros((ROWS, PTS), F32)
    for t in range(4):
        first = jnp.where(segment == t, one_c[t * ROWS : (t + 1) * ROWS], first)
        last = jnp.where(segment == t, one_c[(t + 4) * ROWS : (t + 5) * ROWS], last)
    strip_ref[:ROWS, FIRST] = first
    strip_ref[:ROWS, LAST] = last
    for t in range(4):
        for g in range(8):
            low, high = slice(g * PTS, (g + 1) * PTS), slice(1024 + g * PTS, 1024 + (g + 1) * PTS)
            sums[t * ROWS : (t + 1) * ROWS, low] = (
                two_rows[t : t + 1, low] * one_c[2 * t * ROWS : (2 * t + 1) * ROWS]
                + two_rows[t : t + 1, high] * one_c[(2 * t + 1) * ROWS : (2 * t + 2) * ROWS]
            )
    two = dot_two(sums[: 4 * ROWS], ones)
    top = jnp.zeros((ROWS, PTS), F32)
    for t in range(4):
        top = jnp.where(segment == t, two[t * ROWS : (t + 1) * ROWS], top)
    for copy in range(top_ref.shape[0]):
        top_ref[copy] = top


def couple_kernel(place, lists, mine_ref, other_ref, mats_ref, out_ref, table, sums):
    rank, core = place[0], place[1]
    segment = lane_segment(ROWS)
    half = mine_ref.shape[0]
    table[:half] = mine_ref[...]
    table[half:] = other_ref[...]
    sums[...] = jnp.zeros(sums.shape, F32)

    def body(block, _):
        for t in range(8):
            target = block * 8 + t
            rows = pl.ds(pl.multiple_of(target * ROWS, ROWS), ROWS)
            entries = [lists[target, j] for j in range(COUPLE)]
            lives = [(n >= 0) & (((n >> 2) & 3) == rank) for n in entries]
            for j in range(COUPLE):

                @pl.when(lives[j])
                def _(j=j, n=entries[j]):
                    group = n >> 4
                    coef = pick(table[((group & 1) ^ core) * half + (group >> 1)], segment, n & 3)
                    for g in range(8):
                        row = mats_ref[block, t : t + 1, j * 1024 + g * PTS : j * 1024 + (g + 1) * PTS]
                        sums[rows, g * PTS : (g + 1) * PTS] += row * coef

        return 0

    lax.fori_loop(0, 2, body, 0)
    total = dot_two(sums[...], summing())
    for part in range(4):
        packed = jnp.zeros((ROWS, PTS), F32)
        for t in range(4):
            at = (part * 4 + t) * ROWS
            packed = jnp.where(segment == t, total[at : at + ROWS], packed)
        out_ref[part] = packed


def near_kernel(place, near, left, own, right, out_ref, geo, weights):
    rank, base = place[0], place[2] * OWN - OWN
    zeros = jnp.zeros((PTS, ROWS), BF16)
    for s in range(3 * OWN):
        which, at = divmod(s, OWN)
        ref = (left, own, right)[which]
        cut = slice(at * PTS, (at + 1) * PTS)
        geo[s, 0:3] = ref[ROWS : ROWS + 3, cut]
        geo[s, 3:6] = ref[ROWS + 3 : ROWS + 6, cut] * CONTRAST
        scaled = ref[:ROWS, cut] * ref[ROWS + 6 : ROWS + 7, cut]
        high = scaled.astype(BF16).astype(F32)
        turned = jnp.transpose(jnp.concatenate([high, scaled - high], 0)).astype(BF16)
        weights[s, 0:PTS] = turned
        weights[s, PTS : 2 * PTS] = jnp.concatenate([turned[:, :ROWS], zeros], 1)
    geo[3 * OWN] = jnp.zeros((8, PTS), F32)
    weights[3 * OWN] = jnp.zeros((2 * PTS, 2 * ROWS), BF16)

    def body(i, _):
        at = jnp.transpose(geo[OWN + i])
        px = jnp.broadcast_to(at[:, 0:1], (PTS, PTS))
        py = jnp.broadcast_to(at[:, 1:2], (PTS, PTS))
        pz = jnp.broadcast_to(at[:, 2:3], (PTS, PTS))
        total = jnp.zeros((PTS, 2 * ROWS), F32)
        for j in range(NEAR):
            n = near[rank * OWN + i, j]
            s = jnp.where(n >= 0, jnp.clip(n - base, 0, 3 * OWN - 1), 3 * OWN)
            src = geo[s]
            dx, dy, dz = px - src[0:1], py - src[1:2], pz - src[2:3]
            inv = lax.rsqrt(dx * dx + dy * dy + dz * dz + SOFTEN)
            turn = dx * src[3:4] + dy * src[4:5] + dz * src[5:6]
            value = inv + turn * (inv * inv * inv)
            high, low = split(value)
            total = total + dot(jnp.concatenate([high, low], 1), weights[s])
        flat = jnp.transpose(total)
        out_ref[:, pl.ds(pl.multiple_of(i * PTS, PTS), PTS)] = flat[:ROWS] + flat[ROWS:]
        return 0

    lax.fori_loop(0, OWN, body, 0)


def final_kernel(
    place, lists, parts, left, own, right,
    one_ref, two_ref, mats_ref, basis_ref, near_ref, out_ref, table, sums, spread, two_rows,
):
    rank, base = place[0], place[2] * 8 - 4
    two_rows[...] = own_half(two_ref, rank)
    segment = lane_segment(ROWS)
    for at, (ref, half) in enumerate(((left, 1), (own, 0), (own, 1), (right, 0))):
        table[at] = ref[:, half * PTS : (half + 1) * PTS]

    for t in range(8):
        acc = [None] * 8
        for j in range(COUPLE):
            n = lists[rank * 8 + t, j]
            q = jnp.clip(n - base, 0, 15)
            slot = jnp.where(n >= 0, q & 3, -1)
            coef = pick(table[q >> 2], segment, slot)
            for g in range(8):
                row = mats_ref[t : t + 1, j * 1024 + g * PTS : j * 1024 + (g + 1) * PTS]
                acc[g] = row * coef if j == 0 else acc[g] + row * coef
        for g in range(8):
            sums[t * ROWS : (t + 1) * ROWS, g * PTS : (g + 1) * PTS] = acc[g]
    mid = dot_two(sums[...], summing())
    down = parts[0] + parts[1] + parts[2] + parts[3]
    rows = jnp.concatenate([jnp.where(segment == t, down, 0.0) for t in range(4)], 0)
    spread[: 4 * ROWS] = dot_two(rows, spreading(4))
    mids = []
    for t in range(4):
        for k in range(2):
            acc = None
            for g in range(8):
                lanes = slice(g * PTS, (g + 1) * PTS)
                row = two_rows[t : t + 1, k * 1024 + g * PTS : k * 1024 + (g + 1) * PTS]
                term = row * spread[t * ROWS : (t + 1) * ROWS, lanes]
                acc = term if g == 0 else acc + term
            at = (2 * t + k) * ROWS
            mids.append(mid[at : at + ROWS] + fold(acc))
    spread[...] = dot_two(jnp.concatenate(mids, 0), spreading(1))
    zeros = jnp.zeros((RANK, PTS), BF16)
    for t in range(8):
        for k in range(2):
            acc = None
            for g in range(8):
                lanes = slice(g * PTS, (g + 1) * PTS)
                row = one_ref[t : t + 1, k * 1024 + g * PTS : k * 1024 + (g + 1) * PTS]
                term = row * spread[t * ROWS : (t + 1) * ROWS, lanes]
                acc = term if g == 0 else acc + term
            down_leaf = fold(acc)
            leaf = 2 * t + k
            high = down_leaf.astype(BF16).astype(F32)
            low = down_leaf - high
            lhs = jnp.where(segment == 1, low, jnp.where(segment == 3, 0.0, high)).astype(BF16)
            bh, bl = split(basis_ref[leaf])
            far = dot(lhs, jnp.concatenate([bh, bh, bl, zeros], 0))
            cut = slice(leaf * PTS, (leaf + 1) * PTS)
            out_ref[:, cut] = near_ref[:, cut] + far


def shape(*dims):
    return jax.ShapeDtypeStruct(dims, F32)


def on_device(values, geometry, basis, near, transfer_one, transfer_two, couple_one, couple_two, lists_one, lists_two):
    size = lax.axis_size("x") * lax.axis_size("z") * lax.axis_size("c") * lax.axis_size("r")
    gathered = lax.axis_size("x") * lax.axis_size("z")
    place = jnp.stack([lax.axis_index("r"), lax.axis_index("c"), lax.axis_index(ALL)]).astype(jnp.int32)
    up_by_one = [(i, i + 1) for i in range(size - 1)]
    down_by_one = [(i + 1, i) for i in range(size - 1)]

    val = lax.all_to_all(values, "r", split_axis=1, concat_axis=0, tiled=True)

    def rows_of(height, width):
        return pl.BlockSpec((height, width), lambda i, place: (place[0], 0))

    def whole(*dims):
        return pl.BlockSpec(dims, lambda i, place: (0,) * len(dims))

    two_of = pl.BlockSpec((1, 8, 2048), lambda i, place: (place[0] // 2, 0, 0))
    transfer_two = transfer_two.reshape(2, 8, 2048)
    couple_two = couple_two.reshape(2, 8, 8192)

    strip, top = pl.pallas_call(
        up_kernel,
        grid_spec=pltpu.PrefetchScalarGridSpec(
            num_scalar_prefetch=1,
            grid=(1,),
            in_specs=[whole(ROWS, OWN * PTS), whole(7, OWN * PTS), whole(OWN, RANK, PTS), rows_of(8, 2048), two_of],
            out_specs=[whole(*STRIP), whole(gathered, ROWS, PTS)],
            scratch_shapes=[
                pltpu.VMEM((OWN, ROWS, PTS), F32),
                pltpu.VMEM((8 * ROWS, PTS), F32),
                pltpu.VMEM((8 * ROWS, 1024), F32),
                pltpu.VMEM((8, 2048), F32),
            ],
        ),
        out_shape=[shape(*STRIP), shape(gathered, ROWS, PTS)],
        compiler_params=PARAMS,
        cost_estimate=pl.CostEstimate(flops=40_000_000, bytes_accessed=600_000, transcendentals=0),
    )(place, val, geometry, basis, transfer_one, transfer_two)

    left = lax.ppermute(strip, ALL, up_by_one)
    right = lax.ppermute(strip, ALL, down_by_one)

    mine = lax.all_to_all(top, ("x", "z"), split_axis=0, concat_axis=0, tiled=True)
    other = lax.ppermute(mine, "c", [(0, 1), (1, 0)])

    parts = pl.pallas_call(
        couple_kernel,
        in_specs=[SMEM, SMEM, VMEM, VMEM, VMEM],
        out_specs=VMEM,
        out_shape=shape(4, ROWS, PTS),
        scratch_shapes=[pltpu.VMEM((2 * gathered, ROWS, PTS), F32), pltpu.VMEM((16 * ROWS, 1024), F32)],
        compiler_params=PARAMS,
        cost_estimate=pl.CostEstimate(flops=100_000_000, bytes_accessed=1_000_000, transcendentals=0),
    )(place, lists_two, mine, other, couple_two)
    parts = lax.all_to_all(parts, "r", split_axis=0, concat_axis=0, tiled=True)

    near_part = pl.pallas_call(
        near_kernel,
        in_specs=[SMEM, SMEM] + [VMEM] * 3,
        out_specs=VMEM,
        out_shape=shape(ROWS, OWN * PTS),
        scratch_shapes=[
            pltpu.VMEM((3 * OWN + 1, 8, PTS), F32),
            pltpu.VMEM((3 * OWN + 1, 2 * PTS, 2 * ROWS), BF16),
        ],
        compiler_params=PARAMS,
        cost_estimate=pl.CostEstimate(flops=3_000_000_000, bytes_accessed=700_000, transcendentals=1_600_000),
    )(place, near, left, strip, right)

    result = pl.pallas_call(
        final_kernel,
        grid_spec=pltpu.PrefetchScalarGridSpec(
            num_scalar_prefetch=1,
            grid=(1,),
            in_specs=[SMEM]
            + [whole(4, ROWS, PTS)]
            + [pl.BlockSpec((ROWS, 2 * PTS), lambda i, place: (0, OWN // 2))] * 3
            + [rows_of(8, 2048), two_of, rows_of(8, 8192), whole(OWN, RANK, PTS), whole(ROWS, OWN * PTS)],
            out_specs=whole(ROWS, OWN * PTS),
            scratch_shapes=[
                pltpu.VMEM((4, ROWS, PTS), F32),
                pltpu.VMEM((8 * ROWS, 1024), F32),
                pltpu.VMEM((8 * ROWS, 1024), F32),
                pltpu.VMEM((8, 2048), F32),
            ],
        ),
        out_shape=shape(ROWS, OWN * PTS),
        compiler_params=PARAMS,
        cost_estimate=pl.CostEstimate(flops=40_000_000, bytes_accessed=1_000_000, transcendentals=0),
    )(
        place, lists_one, parts, left, strip, right,
        transfer_one, transfer_two, couple_one, basis, near_part,
    )
    return lax.all_to_all(result, "r", split_axis=0, concat_axis=1, tiled=True)


def solution(mesh):
    fine = Mesh(mesh.devices.reshape(4, 8, 2, 4), ALL)
    leaf = ("x", "z", "c")
    return jax.shard_map(
        on_device,
        mesh=fine,
        in_specs=(
            P("r", leaf),
            P(None, ALL),
            P(ALL, None, None),
            P(leaf, None),
            P(leaf, None),
            P(leaf, None),
            P(leaf, None),
            P(leaf, None),
            P(leaf, None),
            P(leaf, None),
        ),
        out_specs=P("r", leaf),
        check_vma=False,
    )
```

```python
import jax
import jax.numpy as jnp
from jax import lax
from jax.experimental import pallas as pl
from jax.experimental.pallas import tpu as pltpu
from jax.sharding import Mesh
from jax.sharding import PartitionSpec as P

PTS = 128
RANK = 32
NEAR = 6
COUPLE = 8
SOFTEN = 0.05
CONTRAST = 0.6
ROWS = 16
OWN = 16
FIRST = slice(OWN * PTS, OWN * PTS + PTS)
LAST = slice(OWN * PTS + PTS, OWN * PTS + 2 * PTS)
STRIP = (ROWS + 8, OWN * PTS + 2 * PTS)
MESSAGE = OWN * PTS + 2 * PTS + 4 * PTS
F32 = jnp.float32
BF16 = jnp.bfloat16
ALL = ("x", "z", "c", "r")
VMEM = pl.BlockSpec(memory_space=pltpu.VMEM)
ANY = pl.BlockSpec(memory_space=pl.ANY)
SMEM = pl.BlockSpec(memory_space=pltpu.SMEM)
PARAMS = pltpu.CompilerParams(vmem_limit_bytes=40 * 1024 * 1024)


def split(x):
    high = x.astype(BF16)
    return high, (x - high.astype(F32)).astype(BF16)


def dot(a, b):
    return jnp.dot(a, b, preferred_element_type=F32)


def dot_two(x, ones):
    high, low = split(x)
    return dot(high, ones) + dot(low, ones)


def dot_last(a, b):
    return lax.dot_general(a, b, (((1,), (1,)), ((), ())), preferred_element_type=F32)


def lane_segment(rows):
    return lax.broadcasted_iota(jnp.int32, (rows, PTS), 1) >> 5


def fold(x):
    x = x + pltpu.roll(x, 64, 1)
    return x + pltpu.roll(x, 32, 1)


def summing():
    rows = lax.broadcasted_iota(jnp.int32, (1024, PTS), 0) >> 5
    lanes = lax.broadcasted_iota(jnp.int32, (1024, PTS), 1) & 31
    return (rows == lanes).astype(F32).astype(BF16)


def spreading(segments):
    rows = lax.broadcasted_iota(jnp.int32, (PTS, 1024), 0)
    lanes = lax.broadcasted_iota(jnp.int32, (PTS, 1024), 1) >> 5
    return (((rows & 31) == lanes) & (rows < segments * RANK)).astype(F32).astype(BF16)


def pick(packed, segment, slot):
    return fold(jnp.where(segment == slot, packed, 0.0))


def pack(rows, segment):
    packed = rows[:ROWS]
    for t in range(1, 4):
        packed = jnp.where(segment == t, rows[t * ROWS : (t + 1) * ROWS], packed)
    return packed


def up_kernel(
    place, v_ref, geo_hbm, basis_ref, one_hbm, two_hbm, strip_ref, top_ref,
    leaf_c, one_c, sums, geo, one, two, sems,
):
    rank = place[0]
    copies = [
        pltpu.make_async_copy(src, dst, sems.at[at])
        for at, (src, dst) in enumerate(((one_hbm.at[rank], one), (two_hbm.at[rank // 2], two), (geo_hbm, geo)))
    ]
    for copy in copies:
        copy.start()
    segment = lane_segment(ROWS)
    ones = summing()
    zeros = jnp.zeros((2 * RANK, PTS), BF16)
    strip_ref[:ROWS, : OWN * PTS] = v_ref[...]
    for leaf in range(OWN):
        vh, vl = split(v_ref[:, leaf * PTS : (leaf + 1) * PTS])
        bh, bl = split(basis_ref[leaf])
        prod = dot_last(jnp.concatenate([vh, vl], 0), jnp.concatenate([bh, bl, zeros], 0))
        leaf_c[leaf] = fold(prod[:ROWS] + prod[ROWS:])
    copies[0].wait()
    for t in range(8):
        for g in range(8):
            low, high = slice(g * PTS, (g + 1) * PTS), slice(1024 + g * PTS, 1024 + (g + 1) * PTS)
            sums[t * ROWS : (t + 1) * ROWS, low] = (
                one[t : t + 1, low] * leaf_c[2 * t] + one[t : t + 1, high] * leaf_c[2 * t + 1]
            )
    one_c[...] = dot_two(sums[...], ones)
    strip_ref[:ROWS, FIRST] = pack(one_c[: 4 * ROWS], segment)
    strip_ref[:ROWS, LAST] = pack(one_c[4 * ROWS :], segment)
    copies[1].wait()
    two[...] = pltpu.roll(two[...], (rank % 2) * 4, 0)
    for t in range(4):
        for g in range(8):
            low, high = slice(g * PTS, (g + 1) * PTS), slice(1024 + g * PTS, 1024 + (g + 1) * PTS)
            sums[t * ROWS : (t + 1) * ROWS, low] = (
                two[t : t + 1, low] * one_c[2 * t * ROWS : (2 * t + 1) * ROWS]
                + two[t : t + 1, high] * one_c[(2 * t + 1) * ROWS : (2 * t + 2) * ROWS]
            )
    top = pack(dot_two(sums[: 4 * ROWS], ones), segment)
    for copy in range(top_ref.shape[0]):
        top_ref[copy] = top
    copies[2].wait()
    strip_ref[ROWS : ROWS + 7, : OWN * PTS] = geo[...]


def couple_rows(coefs, first, row_of, sums):
    for t in range(sums.shape[0] // ROWS):
        acc = [None] * 8
        for j in range(COUPLE):
            coef = coefs[first + t * COUPLE + j]
            for g in range(8):
                term = row_of(t, slice(j * 1024 + g * PTS, j * 1024 + (g + 1) * PTS)) * coef
                acc[g] = term if j == 0 else acc[g] + term
        for g in range(8):
            sums[t * ROWS : (t + 1) * ROWS, g * PTS : (g + 1) * PTS] = acc[g]


def couple_kernel(place, lists, mine_ref, other_ref, mats_ref, near_ref, out_ref, table, coefs, sums):
    rank, core = place[0], place[1]
    segment = lane_segment(ROWS)
    half = mine_ref.shape[0]
    table[:half] = mine_ref[...]
    table[half:] = other_ref[...]
    for t in range(16):
        for j in range(COUPLE):
            n = lists[t, j]
            live = (n >= 0) & (((n >> 2) & 3) == rank)
            group = jnp.where(live, n >> 4, 0)
            slot = jnp.where(live, n & 3, -1)
            coefs[t * COUPLE + j] = pick(table[((group & 1) ^ core) * half + (group >> 1)], segment, slot)
    couple_rows(coefs, 0, lambda t, lanes: mats_ref[t : t + 1, lanes], sums)
    total = dot_two(sums[...], summing())
    out_ref[:, : OWN * PTS + 2 * PTS] = near_ref[...]
    for part in range(4):
        at = OWN * PTS + (2 + part) * PTS
        out_ref[:, at : at + PTS] = pack(total[part * 4 * ROWS : (part + 1) * 4 * ROWS], segment)


def near_kernel(
    place, near, lists, left, own, right, mats_hbm, out_ref, geo, weights, mats, table, coefs, sums, sem
):
    rank, base = place[0], place[2] * OWN - OWN
    copy = pltpu.make_async_copy(mats_hbm.at[rank], mats, sem)
    copy.start()
    zeros = jnp.zeros((ROWS, PTS), BF16)
    for s in range(3 * OWN):
        which, at = divmod(s, OWN)
        ref = (left, own, right)[which]
        cut = slice(at * PTS, (at + 1) * PTS)
        geo[s, 0:3] = ref[ROWS : ROWS + 3, cut]
        geo[s, 3:6] = ref[ROWS + 3 : ROWS + 6, cut] * CONTRAST
        high, low = split(ref[:ROWS, cut] * ref[ROWS + 6 : ROWS + 7, cut])
        weights[s, :ROWS, :PTS] = high
        weights[s, :ROWS, PTS:] = high
        weights[s, ROWS:, :PTS] = low
        weights[s, ROWS:, PTS:] = zeros
    geo[3 * OWN] = jnp.zeros((8, PTS), F32)
    weights[3 * OWN] = jnp.zeros((2 * ROWS, 2 * PTS), BF16)

    def leaf(i):
        at = jnp.transpose(geo[OWN + i])
        px, py, pz = (jnp.broadcast_to(at[:, k : k + 1], (PTS, PTS)) for k in range(3))
        total = None
        for j in range(NEAR):
            n = near[rank * OWN + i, j]
            s = jnp.where(n >= 0, jnp.clip(n - base, 0, 3 * OWN - 1), 3 * OWN)
            src = geo[s]
            dx, dy, dz = px - src[0:1], py - src[1:2], pz - src[2:3]
            inv = lax.rsqrt(dx * dx + dy * dy + dz * dz + SOFTEN)
            turn = dx * src[3:4] + dy * src[4:5] + dz * src[5:6]
            high, low = split(inv + turn * (inv * inv * inv))
            term = dot_last(jnp.concatenate([high, low], 1), weights[s])
            total = term if j == 0 else total + term
        flat = jnp.transpose(total)
        out_ref[:, pl.ds(pl.multiple_of(i * PTS, PTS), PTS)] = flat[:ROWS] + flat[ROWS:]

    def leaves(step, _):
        for u in range(8):
            leaf(step * 8 + u)
        return 0

    lax.fori_loop(0, OWN // 8, leaves, 0)

    segment = lane_segment(ROWS)
    for at, (ref, lanes) in enumerate(((left, LAST), (own, FIRST), (own, LAST), (right, FIRST))):
        table[at] = ref[:ROWS, lanes]
    first = place[2] * 8 - 4
    for t in range(8):
        for j in range(COUPLE):
            n = lists[rank * 8 + t, j]
            q = jnp.clip(n - first, 0, 15)
            coefs[t * COUPLE + j] = pick(table[q >> 2], segment, jnp.where(n >= 0, q & 3, -1))
    copy.wait()
    couple_rows(coefs, 0, lambda t, lanes: mats[t : t + 1, lanes], sums)
    total = dot_two(sums[...], summing())
    for part in range(2):
        at = OWN * PTS + part * PTS
        out_ref[:, at : at + PTS] = pack(total[part * 4 * ROWS : (part + 1) * 4 * ROWS], segment)


def final_kernel(got, one_ref, two_ref, basis_ref, out_ref, spread_two, spread_one):
    segment = lane_segment(8)
    lower = lax.broadcasted_iota(jnp.int32, (8, PTS), 0) < 4

    def twice(x):
        return jnp.concatenate([x, x], 0)

    def rows_of(ref, t, u, lanes):
        return jnp.where(lower, ref[t : t + 1, lanes], ref[u : u + 1, lanes])

    def apply(ref, t, u, k, spread, at):
        acc = None
        for g in range(8):
            rows = rows_of(ref, t, u, slice(k * 1024 + g * PTS, k * 1024 + (g + 1) * PTS))
            term = rows * spread[at : at + 8, g * PTS : (g + 1) * PTS]
            acc = term if g == 0 else acc + term
        return acc

    start = OWN * PTS + 2 * PTS
    rows = []
    for part in range(4):
        lanes = slice(start + part * PTS, start + (part + 1) * PTS)
        down = twice(got[0, :, lanes] + got[1, :, lanes] + got[2, :, lanes] + got[3, :, lanes])
        for slot in (0, 2):
            rows.append(jnp.where(segment == jnp.where(lower, slot, slot + 1), down, 0.0))
    spread_two[...] = dot_two(jnp.concatenate(rows, 0), spreading(4))
    mids = []
    for m in range(8):
        lanes = slice(OWN * PTS + (m % 2) * PTS, OWN * PTS + (m % 2 + 1) * PTS)
        own = twice(got[m // 2, :, lanes])
        for k in range(2):
            acc = apply(two_ref, 2 * m, 2 * m + 1, k, spread_two, 8 * m)
            mids.append(fold(acc + jnp.where(segment == jnp.where(lower, k, k + 2), own, 0.0)))
    spread_one[...] = dot_two(jnp.concatenate(mids, 0), spreading(1))
    zeros = jnp.zeros((RANK, PTS), BF16)
    for m in range(8):
        for k in range(2):
            t, u = 4 * m + k, 4 * m + k + 2
            for side in range(2):
                down = fold(apply(one_ref, t, u, side, spread_one, (2 * m + k) * 8))
                high = down.astype(BF16).astype(F32)
                lhs = jnp.where(segment == 1, down - high, jnp.where(segment == 3, 0.0, high)).astype(BF16)
                pair = []
                for leaf in (2 * t + side, 2 * u + side):
                    bh, bl = split(basis_ref[leaf])
                    pair.append(jnp.concatenate([bh, bh, bl, zeros], 0))
                far = dot(lhs, jnp.concatenate(pair, 1))
                for leaf, part in ((2 * t + side, far[:4, :PTS]), (2 * u + side, far[4:, PTS:])):
                    at = leaf % OWN * PTS
                    out_ref[:, leaf * PTS : (leaf + 1) * PTS] = got[leaf // OWN, :, at : at + PTS] + part


def shape(*dims):
    return jax.ShapeDtypeStruct(dims, F32)


def scratch(*dims):
    return pltpu.VMEM(dims, F32)


def on_device(values, geometry, basis, near, transfer_one, transfer_two, couple_one, couple_two, lists_one, lists_two):
    size = lax.axis_size("x") * lax.axis_size("z") * lax.axis_size("c") * lax.axis_size("r")
    gathered = lax.axis_size("x") * lax.axis_size("z")
    place = jnp.stack([lax.axis_index("r"), lax.axis_index("c"), lax.axis_index(ALL)]).astype(jnp.int32)

    basis_all = lax.all_gather(basis, "r", axis=0, tiled=True)
    val = lax.all_to_all(values, "r", split_axis=1, concat_axis=0, tiled=True)
    strip, top = pl.pallas_call(
        up_kernel,
        in_specs=[SMEM, VMEM, ANY, VMEM, ANY, ANY],
        out_specs=[VMEM, VMEM],
        out_shape=[shape(*STRIP), shape(gathered, ROWS, PTS)],
        scratch_shapes=[
            scratch(OWN, ROWS, PTS),
            scratch(8 * ROWS, PTS),
            scratch(8 * ROWS, 1024),
            scratch(7, OWN * PTS),
            scratch(8, 2048),
            scratch(8, 2048),
            pltpu.SemaphoreType.DMA((3,)),
        ],
        compiler_params=PARAMS,
        cost_estimate=pl.CostEstimate(flops=40_000_000, bytes_accessed=600_000, transcendentals=0),
    )(place, val, geometry, basis, transfer_one.reshape(4, 8, 2048), transfer_two.reshape(2, 8, 2048))

    left = lax.ppermute(strip, ALL, [(i, i + 1) for i in range(size - 1)])
    right = lax.ppermute(strip, ALL, [(i + 1, i) for i in range(size - 1)])
    mine = lax.all_to_all(top, ("x", "z"), split_axis=0, concat_axis=0, tiled=True)
    other = lax.ppermute(mine, "c", [(0, 1), (1, 0)])

    near_part = pl.pallas_call(
        near_kernel,
        in_specs=[SMEM, SMEM, SMEM, VMEM, VMEM, VMEM, ANY],
        out_specs=VMEM,
        out_shape=shape(ROWS, OWN * PTS + 2 * PTS),
        scratch_shapes=[
            scratch(3 * OWN + 1, 8, PTS),
            pltpu.VMEM((3 * OWN + 1, 2 * ROWS, 2 * PTS), BF16),
            scratch(8, 8192),
            scratch(4, ROWS, PTS),
            scratch(8 * COUPLE, ROWS, PTS),
            scratch(8 * ROWS, 1024),
            pltpu.SemaphoreType.DMA(()),
        ],
        compiler_params=PARAMS,
        cost_estimate=pl.CostEstimate(flops=3_000_000_000, bytes_accessed=700_000, transcendentals=1_600_000),
    )(place, near, lists_one, left, strip, right, couple_one.reshape(4, 8, 8192))

    message = pl.pallas_call(
        couple_kernel,
        in_specs=[SMEM, SMEM, VMEM, VMEM, VMEM, VMEM],
        out_specs=VMEM,
        out_shape=shape(ROWS, MESSAGE),
        scratch_shapes=[
            scratch(2 * gathered, ROWS, PTS),
            scratch(16 * COUPLE, ROWS, PTS),
            scratch(16 * ROWS, 1024),
        ],
        compiler_params=PARAMS,
        cost_estimate=pl.CostEstimate(flops=100_000_000, bytes_accessed=1_000_000, transcendentals=0),
    )(place, lists_two, mine, other, couple_two, near_part)
    got = lax.all_to_all(message.reshape(4, 4, MESSAGE), "r", split_axis=0, concat_axis=0, tiled=True)

    return pl.pallas_call(
        final_kernel,
        in_specs=[VMEM] * 4,
        out_specs=VMEM,
        out_shape=shape(4, 4 * OWN * PTS),
        scratch_shapes=[scratch(64, 1024), scratch(128, 1024)],
        compiler_params=PARAMS,
        cost_estimate=pl.CostEstimate(flops=40_000_000, bytes_accessed=2_000_000, transcendentals=0),
    )(got, transfer_one, transfer_two, basis_all)


def solution(mesh):
    fine = Mesh(mesh.devices.reshape(4, 8, 2, 4), ALL)
    leaf = ("x", "z", "c")
    return jax.shard_map(
        on_device,
        mesh=fine,
        in_specs=(
            P("r", leaf),
            P(None, ALL),
            P(ALL, None, None),
            P(leaf, None),
            P(leaf, None),
            P(leaf, None),
            P(leaf, None),
            P(leaf, None),
            P(leaf, None),
            P(leaf, None),
        ),
        out_specs=P("r", leaf),
        check_vma=False,
    )
```

```python
import jax
import jax.numpy as jnp
from jax import lax
from jax.experimental import pallas as pl
from jax.experimental.pallas import tpu as pltpu
from jax.sharding import Mesh
from jax.sharding import PartitionSpec as P

PTS = 128
RANK = 32
NEAR = 6
COUPLE = 8
SOFTEN = 0.05
CONTRAST = 0.6
ROWS = 16
OWN = 16
FIRST = slice(OWN * PTS, OWN * PTS + PTS)
LAST = slice(OWN * PTS + PTS, OWN * PTS + 2 * PTS)
STRIP = (ROWS + 8, OWN * PTS + 2 * PTS)
MESSAGE = OWN * PTS + 2 * PTS + 4 * PTS
F32 = jnp.float32
BF16 = jnp.bfloat16
ALL = ("x", "z", "c", "r")
VMEM = pl.BlockSpec(memory_space=pltpu.VMEM)
HBM = pl.BlockSpec(memory_space=pltpu.HBM)
SMEM = pl.BlockSpec(memory_space=pltpu.SMEM)
PARAMS = pltpu.CompilerParams(vmem_limit_bytes=16 * 1024 * 1024)


def split(x):
    high = x.astype(BF16)
    return high, (x - high.astype(F32)).astype(BF16)


def dot(a, b):
    return jnp.dot(a, b, preferred_element_type=F32)


def dot_two(x, ones):
    high, low = split(x)
    return dot(high, ones) + dot(low, ones)


def dot_last(a, b):
    return lax.dot_general(a, b, (((1,), (1,)), ((), ())), preferred_element_type=F32)


def lane_segment(rows):
    return lax.broadcasted_iota(jnp.int32, (rows, PTS), 1) >> 5


def fold(x):
    x = x + pltpu.roll(x, 64, 1)
    return x + pltpu.roll(x, 32, 1)


def summing():
    rows = lax.broadcasted_iota(jnp.int32, (1024, PTS), 0) >> 5
    lanes = lax.broadcasted_iota(jnp.int32, (1024, PTS), 1) & 31
    return (rows == lanes).astype(F32).astype(BF16)


def spreading(segments):
    rows = lax.broadcasted_iota(jnp.int32, (PTS, 1024), 0)
    lanes = lax.broadcasted_iota(jnp.int32, (PTS, 1024), 1) >> 5
    return (((rows & 31) == lanes) & (rows < segments * RANK)).astype(F32).astype(BF16)


def pick(packed, segment, slot):
    return fold(jnp.where(segment == slot, packed, 0.0))


def pack(rows, segment):
    packed = rows[:ROWS]
    for t in range(1, 4):
        packed = jnp.where(segment == t, rows[t * ROWS : (t + 1) * ROWS], packed)
    return packed


def block(px, py, pz, src):
    dx, dy, dz = px - src[0:1], py - src[1:2], pz - src[2:3]
    inv = lax.rsqrt(dx * dx + dy * dy + dz * dz + SOFTEN)
    turn = dx * src[3:4] + dy * src[4:5] + dz * src[5:6]
    high, low = split(inv + turn * (inv * inv * inv))
    return jnp.concatenate([high, low], 1)


def prepare_kernel(place, geo_hbm, two_hbm, geo_ref, two_ref, sems):
    rank = place[0]
    copies = [
        pltpu.make_async_copy(geo_hbm, geo_ref.at[pl.ds(0, 7)], sems.at[0]),
        pltpu.make_async_copy(two_hbm.at[rank // 2], two_ref, sems.at[1]),
    ]
    for copy in copies:
        copy.start()
    for copy in copies:
        copy.wait()
    two_ref[...] = pltpu.roll(two_ref[...], (rank % 2) * 4, 0)


def up_kernel(place, v_ref, geo_ref, basis_ref, one_ref, two, strip_ref, top_ref, leaf_c, one_c, sums):
    rank = place[0]
    segment = lane_segment(ROWS)
    ones = summing()
    zeros = jnp.zeros((2 * RANK, PTS), BF16)
    strip_ref[:ROWS, : OWN * PTS] = v_ref[...]
    for leaf in range(OWN):
        vh, vl = split(v_ref[:, leaf * PTS : (leaf + 1) * PTS])
        bh, bl = split(basis_ref[leaf])
        prod = dot_last(jnp.concatenate([vh, vl], 0), jnp.concatenate([bh, bl, zeros], 0))
        leaf_c[leaf] = fold(prod[:ROWS] + prod[ROWS:])
    for t in range(8):
        for g in range(8):
            low, high = slice(g * PTS, (g + 1) * PTS), slice(1024 + g * PTS, 1024 + (g + 1) * PTS)
            sums[t * ROWS : (t + 1) * ROWS, low] = (
                one_ref[rank, t : t + 1, low] * leaf_c[2 * t] + one_ref[rank, t : t + 1, high] * leaf_c[2 * t + 1]
            )
    one_c[...] = dot_two(sums[...], ones)
    strip_ref[:ROWS, FIRST] = pack(one_c[: 4 * ROWS], segment)
    strip_ref[:ROWS, LAST] = pack(one_c[4 * ROWS :], segment)
    for t in range(4):
        for g in range(8):
            low, high = slice(g * PTS, (g + 1) * PTS), slice(1024 + g * PTS, 1024 + (g + 1) * PTS)
            sums[t * ROWS : (t + 1) * ROWS, low] = (
                two[t : t + 1, low] * one_c[2 * t * ROWS : (2 * t + 1) * ROWS]
                + two[t : t + 1, high] * one_c[(2 * t + 1) * ROWS : (2 * t + 2) * ROWS]
            )
    top = pack(dot_two(sums[: 4 * ROWS], ones), segment)
    for copy in range(top_ref.shape[0]):
        top_ref[copy] = top
    strip_ref[ROWS:, : OWN * PTS] = geo_ref[...]


def couple_rows(coefs, first, row_of, sums):
    for t in range(sums.shape[0] // ROWS):
        acc = [None] * 8
        for j in range(COUPLE):
            coef = coefs[first + t * COUPLE + j]
            for g in range(8):
                term = row_of(t, slice(j * 1024 + g * PTS, j * 1024 + (g + 1) * PTS)) * coef
                acc[g] = term if j == 0 else acc[g] + term
        for g in range(8):
            sums[t * ROWS : (t + 1) * ROWS, g * PTS : (g + 1) * PTS] = acc[g]


def couple_kernel(place, lists, mine_ref, other_ref, mats_ref, near_ref, out_ref, table, coefs, sums):
    rank, core = place[0], place[1]
    segment = lane_segment(ROWS)
    half = mine_ref.shape[0]
    table[:half] = mine_ref[...]
    table[half:] = other_ref[...]
    for t in range(16):
        for j in range(COUPLE):
            n = lists[j, t]
            live = (n >= 0) & (((n >> 2) & 3) == rank)
            group = jnp.where(live, n >> 4, 0)
            slot = jnp.where(live, n & 3, -1)
            coefs[t * COUPLE + j] = pick(table[((group & 1) ^ core) * half + (group >> 1)], segment, slot)
    couple_rows(coefs, 0, lambda t, lanes: mats_ref[t : t + 1, lanes], sums)
    total = dot_two(sums[...], summing())
    out_ref[:, : OWN * PTS + 2 * PTS] = near_ref[...]
    for part in range(4):
        at = OWN * PTS + (2 + part) * PTS
        out_ref[:, at : at + PTS] = pack(total[part * 4 * ROWS : (part + 1) * 4 * ROWS], segment)


def near_kernel(
    place, near, lists, left, own, right, mats_hbm, out_ref, geo, weights, mats, table, coefs, sums, sem
):
    rank, base = place[0], place[2] * OWN - OWN
    copy = pltpu.make_async_copy(mats_hbm.at[rank], mats, sem)
    copy.start()
    zeros = jnp.zeros((ROWS, PTS), BF16)
    for s in range(3 * OWN):
        which, at = divmod(s, OWN)
        ref = (left, own, right)[which]
        cut = slice(at * PTS, (at + 1) * PTS)
        geo[s, 0:3] = ref[ROWS : ROWS + 3, cut]
        geo[s, 3:6] = ref[ROWS + 3 : ROWS + 6, cut] * CONTRAST
        high, low = split(ref[:ROWS, cut] * ref[ROWS + 6 : ROWS + 7, cut])
        weights[s, :ROWS, :PTS] = high
        weights[s, :ROWS, PTS:] = high
        weights[s, ROWS:, :PTS] = low
        weights[s, ROWS:, PTS:] = zeros
    geo[3 * OWN] = jnp.zeros((8, PTS), F32)
    weights[3 * OWN] = jnp.zeros((2 * ROWS, 2 * PTS), BF16)

    def leaf(i):
        at = jnp.transpose(geo[OWN + i])
        spots = [jnp.broadcast_to(at[:, k : k + 1], (PTS, PTS)) for k in range(3)]
        total = dot_last(block(*spots, geo[OWN + i]), weights[OWN + i])
        for j in range(1, NEAR):
            n = near[j, rank * OWN + i]
            s = jnp.where(n >= 0, jnp.clip(n - base, 0, 3 * OWN - 1), 3 * OWN)
            total = total + dot_last(block(*spots, geo[s]), weights[s])
        flat = jnp.transpose(total)
        out_ref[:, pl.ds(pl.multiple_of(i * PTS, PTS), PTS)] = flat[:ROWS] + flat[ROWS:]

    def leaves(step, _):
        for u in range(8):
            leaf(step * 8 + u)
        return 0

    lax.fori_loop(0, OWN // 8, leaves, 0)

    segment = lane_segment(ROWS)
    for at, (ref, lanes) in enumerate(((left, LAST), (own, FIRST), (own, LAST), (right, FIRST))):
        table[at] = ref[:ROWS, lanes]
    first = place[2] * 8 - 4
    for t in range(8):
        for j in range(COUPLE):
            n = lists[j, rank * 8 + t]
            q = jnp.clip(n - first, 0, 15)
            coefs[t * COUPLE + j] = pick(table[q >> 2], segment, jnp.where(n >= 0, q & 3, -1))
    copy.wait()
    couple_rows(coefs, 0, lambda t, lanes: mats[t : t + 1, lanes], sums)
    total = dot_two(sums[...], summing())
    for part in range(2):
        at = OWN * PTS + part * PTS
        out_ref[:, at : at + PTS] = pack(total[part * 4 * ROWS : (part + 1) * 4 * ROWS], segment)


def final_kernel(place, got, one_ref, two_ref, basis0, basis1, basis2, basis3, out_ref, spread_two, spread_one, basis_ref):
    for s, ref in enumerate((basis0, basis1, basis2, basis3)):
        basis_ref[pl.ds((place[0] ^ s) * OWN, OWN)] = ref[...]
    segment = lane_segment(8)
    lower = lax.broadcasted_iota(jnp.int32, (8, PTS), 0) < 4

    def twice(x):
        return jnp.concatenate([x, x], 0)

    def rows_of(ref, t, u, lanes):
        return jnp.where(lower, ref[t : t + 1, lanes], ref[u : u + 1, lanes])

    def apply(ref, t, u, k, spread, at):
        acc = None
        for g in range(8):
            rows = rows_of(ref, t, u, slice(k * 1024 + g * PTS, k * 1024 + (g + 1) * PTS))
            term = rows * spread[at : at + 8, g * PTS : (g + 1) * PTS]
            acc = term if g == 0 else acc + term
        return acc

    start = OWN * PTS + 2 * PTS
    rows = []
    for part in range(4):
        lanes = slice(start + part * PTS, start + (part + 1) * PTS)
        down = twice(got[0, :, lanes] + got[1, :, lanes] + got[2, :, lanes] + got[3, :, lanes])
        for slot in (0, 2):
            rows.append(jnp.where(segment == jnp.where(lower, slot, slot + 1), down, 0.0))
    spread_two[...] = dot_two(jnp.concatenate(rows, 0), spreading(4))
    mids = []
    for m in range(8):
        lanes = slice(OWN * PTS + (m % 2) * PTS, OWN * PTS + (m % 2 + 1) * PTS)
        own = twice(got[m // 2, :, lanes])
        for k in range(2):
            acc = apply(two_ref, 2 * m, 2 * m + 1, k, spread_two, 8 * m)
            mids.append(fold(acc + jnp.where(segment == jnp.where(lower, k, k + 2), own, 0.0)))
    spread_one[...] = dot_two(jnp.concatenate(mids, 0), spreading(1))
    zeros = jnp.zeros((RANK, PTS), BF16)
    for m in range(8):
        for k in range(2):
            t, u = 4 * m + k, 4 * m + k + 2
            for side in range(2):
                down = fold(apply(one_ref, t, u, side, spread_one, (2 * m + k) * 8))
                high = down.astype(BF16).astype(F32)
                lhs = jnp.where(segment == 1, down - high, jnp.where(segment == 3, 0.0, high)).astype(BF16)
                pair = []
                for leaf in (2 * t + side, 2 * u + side):
                    bh, bl = split(basis_ref[leaf])
                    pair.append(jnp.concatenate([bh, bh, bl, zeros], 0))
                far = dot(lhs, jnp.concatenate(pair, 1))
                for leaf, part in ((2 * t + side, far[:4, :PTS]), (2 * u + side, far[4:, PTS:])):
                    at = leaf % OWN * PTS
                    out_ref[:, leaf * PTS : (leaf + 1) * PTS] = got[leaf // OWN, :, at : at + PTS] + part


def shape(*dims):
    return jax.ShapeDtypeStruct(dims, F32)


def scratch(*dims):
    return pltpu.VMEM(dims, F32)


def on_device(values, geometry, basis, near, transfer_one, transfer_two, couple_one, couple_two, lists_one, lists_two):
    size = lax.axis_size("x") * lax.axis_size("z") * lax.axis_size("c") * lax.axis_size("r")
    gathered = lax.axis_size("x") * lax.axis_size("z")
    place = jnp.stack([lax.axis_index("r"), lax.axis_index("c"), lax.axis_index(ALL)]).astype(jnp.int32)

    bases = [basis] + [lax.ppermute(basis, "r", [(i, i ^ s) for i in range(4)]) for s in range(1, 4)]
    val = lax.all_to_all(values, "r", split_axis=1, concat_axis=0, tiled=True)
    geo, two = pl.pallas_call(
        prepare_kernel,
        in_specs=[SMEM, HBM, HBM],
        out_specs=[VMEM] * 2,
        out_shape=[shape(8, OWN * PTS), shape(8, 2048)],
        scratch_shapes=[pltpu.SemaphoreType.DMA((2,))],
        compiler_params=PARAMS,
        cost_estimate=pl.CostEstimate(flops=1_000_000, bytes_accessed=300_000, transcendentals=0),
    )(place, geometry, transfer_two.reshape(2, 8, 2048))
    strip, top = pl.pallas_call(
        up_kernel,
        in_specs=[SMEM] + [VMEM] * 5,
        out_specs=[VMEM, VMEM],
        out_shape=[shape(*STRIP), shape(gathered, ROWS, PTS)],
        scratch_shapes=[scratch(OWN, ROWS, PTS), scratch(8 * ROWS, PTS), scratch(8 * ROWS, 1024)],
        compiler_params=PARAMS,
        cost_estimate=pl.CostEstimate(flops=40_000_000, bytes_accessed=600_000, transcendentals=0),
    )(place, val, geo, basis, transfer_one.reshape(4, 8, 2048), two)

    left = lax.ppermute(strip, ALL, [(i, i + 1) for i in range(size - 1)])
    right = lax.ppermute(strip, ALL, [(i + 1, i) for i in range(size - 1)])
    mine = lax.all_to_all(top, ("x", "z"), split_axis=0, concat_axis=0, tiled=True)
    other = lax.ppermute(mine, "c", [(0, 1), (1, 0)])

    near_part = pl.pallas_call(
        near_kernel,
        in_specs=[SMEM] * 3 + [VMEM] * 3 + [HBM],
        out_specs=VMEM,
        out_shape=shape(ROWS, OWN * PTS + 2 * PTS),
        scratch_shapes=[
            scratch(3 * OWN + 1, 8, PTS),
            pltpu.VMEM((3 * OWN + 1, 2 * ROWS, 2 * PTS), BF16),
            scratch(8, 8192),
            scratch(4, ROWS, PTS),
            scratch(8 * COUPLE, ROWS, PTS),
            scratch(8 * ROWS, 1024),
            pltpu.SemaphoreType.DMA(()),
        ],
        compiler_params=PARAMS,
        cost_estimate=pl.CostEstimate(flops=30_000_000_000, bytes_accessed=700_000, transcendentals=1_600_000),
    )(place, near.T, lists_one.T, left, strip, right, couple_one.reshape(4, 8, 8192))

    message = pl.pallas_call(
        couple_kernel,
        in_specs=[SMEM, SMEM, VMEM, VMEM, VMEM, VMEM],
        out_specs=VMEM,
        out_shape=shape(ROWS, MESSAGE),
        scratch_shapes=[
            scratch(2 * gathered, ROWS, PTS),
            scratch(16 * COUPLE, ROWS, PTS),
            scratch(16 * ROWS, 1024),
        ],
        compiler_params=PARAMS,
        cost_estimate=pl.CostEstimate(flops=100_000_000, bytes_accessed=1_000_000, transcendentals=0),
    )(place, lists_two.T, mine, other, couple_two, near_part)
    got = lax.all_to_all(message.reshape(4, 4, MESSAGE), "r", split_axis=0, concat_axis=0, tiled=True)

    return pl.pallas_call(
        final_kernel,
        in_specs=[SMEM] + [VMEM] * 7,
        out_specs=VMEM,
        out_shape=shape(4, 4 * OWN * PTS),
        scratch_shapes=[scratch(64, 1024), scratch(128, 1024), scratch(4 * OWN, RANK, PTS)],
        compiler_params=PARAMS,
        cost_estimate=pl.CostEstimate(flops=40_000_000, bytes_accessed=2_000_000, transcendentals=0),
    )(place, got, transfer_one, transfer_two, *bases)


def solution(mesh):
    fine = Mesh(mesh.devices.reshape(4, 8, 2, 4), ALL)
    leaf = ("x", "z", "c")
    return jax.shard_map(
        on_device,
        mesh=fine,
        in_specs=(
            P("r", leaf),
            P(None, ALL),
            P(ALL, None, None),
            P(leaf, None),
            P(leaf, None),
            P(leaf, None),
            P(leaf, None),
            P(leaf, None),
            P(leaf, None),
            P(leaf, None),
        ),
        out_specs=P("r", leaf),
        check_vma=False,
    )
```
